256 devices in a mesh: source: 8 (over z_hi, y), profile: 8 (over z_lo, core), line: 4 (over x).
Axes of the slice: x: 4, y: 4, z: 8 (z_hi: 2, z_lo: 4; z = z_hi * 4 + z_lo), core: 2. Of those that a mesh axis runs over, the one named last changes fastest.
Arguments:
- source_grad: bfloat16 [8, 3, 256, 256, 512], P('source', None, 'profile', 'line'), may hold values from -30 to 30
- adjoint_grad: bfloat16 [8, 3, 256, 256, 512], P('source', None, 'profile', 'line'), may hold values from -6 to 6
- log_model: float32 [256, 256, 512], P('profile', 'line'), may hold values from -3 to 3
- surface_depth: int32 [256, 256], P('profile', 'line'), may hold values from 0 to 63
- source_columns: int32 [8], replicated, may hold values from 0 to 65535
- receiver_columns: int32 [256], replicated, may hold values from 0 to 65535
Outputs:
- search_direction: float32 [256, 256, 512], P('profile', 'line')
The draws below stay inside these ranges and needn't reach their ends.
All inputs are finite; a program needn't handle non-finite values.
Results may differ from the reference program's by a relative error of at most 0.0003.
Values sent between devices are 32-bit elements; how exact they have to be, the bound alone decides.
No kernel may reach another device: no remote copies, remote signals or barrier semaphores. Data moves between devices by JAX's collectives and lax.ppermute only.
A program may use at most 128 MiB of HBM per device.

```python
import jax
import jax.numpy as jnp
from jax import lax

NZ = 512
RECEIVERS = 256
NX = 256
NY = 256
SOURCES = 8


def field_values(key, spread):
    first, second = jax.random.split(key, 2)
    shape = (SOURCES, 3, NX, NY, NZ)
    base = jax.random.truncated_normal(first, -5.0, 5.0, shape, jnp.float32)
    scale = jnp.exp(jax.random.uniform(second, shape, jnp.float32, -spread, spread))
    return (base * scale).astype(jnp.bfloat16)


def draw_source_grad(key, part):
    key = jax.random.fold_in(key, 11)
    return field_values(key, 1.2)


def plant(array, own_key, smallest, high):
    longest = array.shape.index(max(array.shape))
    spots = []
    for shift in (0, 1):
        where = [jax.random.randint(jax.random.fold_in(own_key, axis), (), 0, length) for axis, length in enumerate(array.shape)]
        where[longest] = (where[longest] + shift) % array.shape[longest]
        spots.append(tuple(where))
    return array.at[spots[0]].set(smallest).at[spots[1]].set(high)


def block_levels(key, shape, shards, smallest, largest):
    def one(axis_at, parts):
        steps = jax.random.uniform(jax.random.fold_in(jax.random.fold_in(key, 6), axis_at), (parts,), jnp.float32, smallest / len(shards), largest / len(shards))
        return jnp.repeat(jnp.exp(steps), shape[axis_at] // parts).reshape((-1,) + (1,) * (len(shape) - axis_at - 1))

    gain = one(*shards[0])
    for cut in shards[1:]:
        gain = gain * one(*cut)
    return gain


def gaussian(rng, shape, scale, most, cuts=(), kind=jnp.bfloat16):
    factor_of = block_levels(rng, shape, cuts, -0.22, 0.18) if cuts else 1.0
    array = jax.random.normal(rng, shape, jnp.float32) * scale * factor_of
    return jnp.minimum(jnp.maximum(array, -most), most).astype(kind)


def setup_inputs(seed: int = 0) -> dict:
    arg_keys = jax.random.split(jax.random.key(seed), 7)
    return {
        "source_grad": draw_source_grad(jax.random.fold_in(arg_keys[6], 71), 0),
        "adjoint_grad": gaussian(arg_keys[1], (SOURCES, 3, NX, NY, NZ), 1.0, 6.0, ((0, 8), (2, 8), (3, 4))),
        "log_model": gaussian(arg_keys[2], (NX, NY, NZ), 0.5, 3.0, ((0, 8), (1, 4)), jnp.float32),
        "surface_depth": plant(jax.random.randint(arg_keys[3], (NX, NY), 0, NZ // 8), jax.random.fold_in(arg_keys[3], 1), 0, (NZ // 8) - 1).astype(jnp.int32),
        "source_columns": plant(jax.random.randint(arg_keys[4], (SOURCES,), 0, NX * NY), jax.random.fold_in(arg_keys[4], 1), 0, (NX * NY) - 1).astype(jnp.int32),
        "receiver_columns": plant(jax.random.randint(arg_keys[5], (RECEIVERS,), 0, NX * NY), jax.random.fold_in(arg_keys[5], 1), 0, (NX * NY) - 1).astype(jnp.int32),
    }


smoothing_rate = 0.15
support_width = 0.3
floor_eps = 1e-06
mark_radius = 3

def diffuse(framed_field, framed_weight):
    centre = framed_field[1:-1, 1:-1]
    weight_mid = framed_weight[1:-1, 1:-1]
    depth_field = jnp.pad(centre, ((0, 0), (0, 0), (1, 1)))
    depth_weight = jnp.pad(weight_mid, ((0, 0), (0, 0), (1, 1)))
    neighbour_pairs = ((framed_field[2:, 1:-1], framed_weight[2:, 1:-1]), (framed_field[:-2, 1:-1], framed_weight[:-2, 1:-1]), (framed_field[1:-1, 2:], framed_weight[1:-1, 2:]), (framed_field[1:-1, :-2], framed_weight[1:-1, :-2]), (depth_field[:, :, 2:], depth_weight[:, :, 2:]), (depth_field[:, :, :-2], depth_weight[:, :, :-2]))
    flux_total = jnp.zeros_like(centre)
    for neighbour, weight_nb in neighbour_pairs:
        flux_total = flux_total + jnp.sqrt(weight_mid * weight_nb) * (neighbour - centre)
    return centre + smoothing_rate * flux_total

def reference(source_grad, adjoint_grad, log_model, surface_depth, source_columns, receiver_columns):

    def accumulate(carry, pair_fields):
        forward = pair_fields[0].astype(jnp.float32)
        backward = pair_fields[1].astype(jnp.float32)
        inner = forward[0] * backward[0] + forward[1] * backward[1] + forward[2] * backward[2]
        forward_sq = forward[0] * forward[0] + forward[1] * forward[1] + forward[2] * forward[2]
        backward_sq = backward[0] * backward[0] + backward[1] * backward[1] + backward[2] * backward[2]
        return ((carry[0] + inner, carry[1] + forward_sq * backward_sq), None)
    zeros_field = jnp.zeros((NX, NY, NZ), jnp.float32)
    (correlation, energy), _ = lax.scan(accumulate, (zeros_field, zeros_field), (source_grad, adjoint_grad))
    scaled = correlation / jnp.sqrt(energy + floor_eps)
    depth_index = lax.broadcasted_iota(jnp.int32, (NX, NY, NZ), 2)
    active = (depth_index >= surface_depth[:, :, None]).astype(jnp.float32)
    columns = jnp.concatenate([source_columns, receiver_columns]).astype(jnp.int32)
    electrode_x = columns // NY
    electrode_y = columns % NY
    grid_x = lax.broadcasted_iota(jnp.int32, (1, NX), 1)
    grid_y = lax.broadcasted_iota(jnp.int32, (1, NY), 1)
    near_x = (jnp.abs(grid_x - electrode_x[:, None]) <= mark_radius).astype(jnp.float32)
    near_y = (jnp.abs(grid_y - electrode_y[:, None]) <= mark_radius).astype(jnp.float32)
    covered = jnp.einsum('ex,ey->xy', near_x, near_y, precision=lax.Precision.HIGHEST)
    band_depth = NZ // 16
    shallow = (depth_index < surface_depth[:, :, None] + band_depth).astype(jnp.float32)
    electrode_marks = (covered > 0.5).astype(jnp.float32)[:, :, None] * shallow
    direction = scaled * active * (1.0 - electrode_marks)
    weight = active * (support_width * support_width) / (log_model * log_model + support_width * support_width)
    framed_weight = jnp.pad(weight, ((1, 1), (1, 1), (0, 0)))
    for sweep_index in range(2):
        direction = diffuse(jnp.pad(direction, ((1, 1), (1, 1), (0, 0))), framed_weight)
    return direction
```

```python
import functools

import jax
import jax.numpy as jnp
import numpy as np
from jax import lax
from jax.experimental import pallas as pl
from jax.experimental.pallas import tpu as pltpu
from jax.sharding import PartitionSpec as P

smoothing_rate = 0.15
support_width = 0.3
floor_eps = 1e-06
mark_radius = 3
ROWS = 16
RIM = 2
PAD = 8

UP = [(4 * z + y, 4 * z + (y + 1) % 4) for z in range(2) for y in range(4)]
DOWN = [(j, i) for i, j in UP]
SWAP = [(4 * z + y, 4 * (1 - z) + y) for z in range(2) for y in range(4)]


def send(x, pairs):
    return lax.ppermute(x, "source", pairs)


def block_lists(tile_x, tile_y):
    groups = tile_y // ROWS
    every = [(p, g) for p in range(tile_x) for g in range(groups)]
    inner = [(p, g) for p, g in every if 4 <= p < tile_x - 4 and 0 < g < groups - 1]
    outer = [b for b in every if b not in inner]
    return [outer, inner]


def tables(blocks):
    arr = np.array(blocks, np.int32)
    return jnp.asarray(arr[:, 0]), jnp.asarray(arr[:, 1])


def vmem(n):
    return [pl.BlockSpec(memory_space=pltpu.VMEM)] * n


def smem(n):
    return [pl.BlockSpec(memory_space=pltpu.SMEM)] * n


def partials(source_grad, adjoint_grad, blocks, starts, count):
    planes, groups = tables(blocks)
    depth = source_grad.shape[-1]
    n = len(starts)

    def body(start_ref, plane_ref, group_ref, *refs):
        for k in range(n):
            f = refs[k][0, :, 0].astype(jnp.float32)
            b = refs[n + k][0, :, 0].astype(jnp.float32)
            out = refs[2 * n + k]
            out[0, 0] = f[0] * b[0] + f[1] * b[1] + f[2] * b[2]
            out[1, 0] = (f[0] * f[0] + f[1] * f[1] + f[2] * f[2]) * (b[0] * b[0] + b[1] * b[1] + b[2] * b[2])

    def spec(k):
        def index(i, start, plane, group):
            at = start[k] + i
            return 0, 0, plane[at], group[at], 0

        return pl.BlockSpec((1, 3, 1, ROWS, depth), index)

    return pl.pallas_call(
        body,
        grid_spec=pltpu.PrefetchScalarGridSpec(
            num_scalar_prefetch=3,
            grid=(count,),
            in_specs=[spec(k) for k in range(n)] * 2,
            out_specs=[pl.BlockSpec((2, 1, ROWS, depth), lambda i, *_: (0, i, 0, 0))] * n,
        ),
        out_shape=[jax.ShapeDtypeStruct((2, count, ROWS, depth), jnp.float32)] * n,
        compiler_params=pltpu.CompilerParams(vmem_limit_bytes=32 * 2**20),
        name="partials",
    )(jnp.stack(starts).astype(jnp.int32), planes, groups, *([source_grad] * n), *([adjoint_grad] * n))


def place(pieces, starts_ref, plane_ref, group_ref, ms_ref, g_ref):
    for k, piece in enumerate(pieces):

        def one(i, _, k=k, piece=piece):
            at = starts_ref[k] + i
            p, g = plane_ref[at], group_ref[at]
            rows = pl.multiple_of(g * ROWS, ROWS)
            g_ref[p + RIM, pl.ds(pl.multiple_of(PAD + rows, 8), ROWS), :] = (
                piece[i] * ms_ref[p, pl.ds(rows, ROWS), :]
            )
            return 0

        lax.fori_loop(0, piece.shape[0], one, 0, unroll=True)


def frame_kernel(n, starts, planes, groups, *refs):
    pieces, (ms, g, low, high) = refs[:n], refs[n:]
    rows = ms.shape[1]
    zero = jnp.zeros((PAD, g.shape[2]), jnp.float32)

    def clear(p, _):
        g[p, :PAD] = zero
        g[p, PAD + rows :] = zero
        return 0

    lax.fori_loop(0, g.shape[0], clear, 0)
    place(pieces, starts, planes, groups, ms, g)

    def rim(p, _):
        low[p] = g[p + RIM, PAD : PAD + RIM]
        high[p] = g[p + RIM, PAD + rows - RIM : PAD + rows]
        return 0

    lax.fori_loop(0, ms.shape[0], rim, 0)


def rim_kernel(g_in, before, after, g, low, high):
    planes = before.shape[0]
    rows = g.shape[1] - 2 * PAD

    def fill(p, _):
        g[p + RIM] = g_in[p + RIM]
        g[p + RIM, PAD - RIM : PAD] = before[p]
        g[p + RIM, PAD + rows : PAD + rows + RIM] = after[p]
        return 0

    lax.fori_loop(0, planes, fill, 0)
    low[...] = g[RIM : 2 * RIM]
    high[...] = g[planes : planes + RIM]


def neighbours(ref, p):
    here = ref[p]
    rows, depth = here.shape
    lane = lax.broadcasted_iota(jnp.int32, here.shape, 1)
    total = ref[p + 1] + ref[p - 1]
    total = total + pltpu.roll(here, 1, 0) + pltpu.roll(here, rows - 1, 0)
    total = total + jnp.where(lane == depth - 1, 0.0, pltpu.roll(here, depth - 1, 1))
    total = total + jnp.where(lane == 0, 0.0, pltpu.roll(here, 1, 1))
    return here, total


def coefficient_kernel(s, a, t):
    planes, rows = t.shape[:2]

    def one(p, _):
        here, total = neighbours(s, p)
        value = 1.0 - smoothing_rate * here * total
        a[p] = value
        return 0

    lax.fori_loop(1, planes + 2 * RIM - 1, one, 0)

    def two(p, _):
        here = s[p + RIM, PAD : PAD + rows]
        value = a[p + RIM, PAD : PAD + rows]
        t[p] = jnp.where(here > 0.0, value / jnp.where(here > 0.0, here, 1.0), 0.0)
        return 0

    lax.fori_loop(0, planes, two, 0)


def smooth_kernel(n, starts, planes, groups, *refs):
    pieces, (ms, s, a, t, low, high, g_in, out, g, g1) = refs[:n], refs[n:]
    count, rows = out.shape[:2]

    def copy(p, _):
        g[p + RIM] = g_in[p + RIM]
        return 0

    lax.fori_loop(0, count, copy, 0)
    place(pieces, starts, planes, groups, ms, g)
    g[:RIM] = low[...]
    g[count + RIM :] = high[...]

    def first(p, _):
        here, total = neighbours(g, p)
        w = s[p]
        g1[p] = a[p] * here + smoothing_rate * w * w * total
        return 0

    lax.fori_loop(1, count + 2 * RIM - 1, first, 0)

    def second(p, _):
        here, total = neighbours(g1, p + RIM)
        inside = slice(PAD, PAD + rows)
        out[p] = t[p] * here[inside] + smoothing_rate * s[p + RIM, PAD : PAD + rows] * total[inside]
        return 0

    lax.fori_loop(0, count, second, 0)


def halo(low, high, axis):
    size = lax.axis_size(axis)
    up = [(i, i + 1) for i in range(size - 1)]
    return lax.ppermute(high, axis, up), lax.ppermute(low, axis, [(j, i) for i, j in up])


def framed(array):
    before, after = halo(array[:, :RIM], array[:, -RIM:], "line")
    fill = jnp.zeros((array.shape[0], PAD - RIM, array.shape[2]), array.dtype)
    wide = jnp.concatenate([fill, before, array, after, fill], axis=1)
    before, after = halo(wide[:RIM], wide[-RIM:], "profile")
    return jnp.concatenate([before, wide, after], axis=0)


def shards(source_grad, adjoint_grad, log_model, surface_depth, source_columns, receiver_columns):
    tile_x, tile_y, depth_cells = log_model.shape
    me = lax.axis_index("source")
    y, half = me % 4, me // 4
    lists = block_lists(tile_x, tile_y)

    def start_of(blocks, offset, z):
        part = len(blocks) // 8
        return (2 * ((y + offset) % 4) + z) * part

    reduced = []
    for blocks in lists:
        part = len(blocks) // 8
        at = functools.partial(start_of, blocks)
        far0, far1 = partials(source_grad, adjoint_grad, blocks, [at(2, 0), at(2, 1)], part)
        near_up, near_down, keep_down, keep_up, own0, own1 = partials(
            source_grad, adjoint_grad, blocks, [at(1, 0), at(-1, 1), at(-1, 0), at(1, 1), at(0, 0), at(0, 1)], part
        )
        far0 = send(far0, DOWN)
        far1 = send(far1, UP)
        got0 = send(near_up, UP)
        got1 = send(near_down, DOWN)
        got0b = send(keep_down + far0, DOWN)
        got1b = send(keep_up + far1, UP)
        own0 = own0 + got0 + got0b
        own1 = own1 + got1 + got1b
        other = send(jnp.where(half == 0, own1, own0), SWAP)
        total = jnp.where(half == 0, own0, own1) + other
        reduced.append(total[0] * lax.rsqrt(total[1] + floor_eps))

    depth_index = lax.broadcasted_iota(jnp.int32, (tile_x, tile_y, depth_cells), 2)
    total_y = tile_y * lax.axis_size("line")
    columns = jnp.concatenate([source_columns, receiver_columns])
    electrode_x = columns // total_y
    electrode_y = columns % total_y
    global_x = lax.broadcasted_iota(jnp.int32, (1, tile_x), 1) + lax.axis_index("profile") * tile_x
    global_y = lax.broadcasted_iota(jnp.int32, (1, tile_y), 1) + lax.axis_index("line") * tile_y
    near_x = (jnp.abs(global_x - electrode_x[:, None]) <= mark_radius).astype(jnp.float32)
    near_y = (jnp.abs(global_y - electrode_y[:, None]) <= mark_radius).astype(jnp.float32)
    covered = jnp.einsum("ex,ey->xy", near_x, near_y, precision=lax.Precision.HIGHEST)
    threshold = surface_depth + jnp.where(covered > 0.5, depth_cells // 16, 0)
    root = support_width * lax.rsqrt(log_model * log_model + support_width * support_width)
    root = jnp.where(depth_index >= surface_depth[:, :, None], root, 0.0)
    masked = jnp.where(depth_index >= threshold[:, :, None], root, 0.0)
    s = framed(root)
    wide = jax.ShapeDtypeStruct(s.shape, jnp.float32)
    tile = jax.ShapeDtypeStruct(log_model.shape, jnp.float32)
    big = pltpu.CompilerParams(vmem_limit_bytes=56 * 2**20)
    a, t = pl.pallas_call(
        coefficient_kernel, out_shape=(wide, tile), in_specs=vmem(1), out_specs=vmem(2), compiler_params=big, name="coefficients"
    )(s)

    def ring(piece):
        cut = piece.shape[0] // 2
        below, above = send(piece, UP), send(piece, DOWN)
        return [piece, below, above, send(below[:cut], UP), send(above[cut:], DOWN)]

    def places(blocks, z):
        cut = len(blocks) // 16
        at = functools.partial(start_of, blocks)
        return [at(0, z), at(-1, z), at(1, z), at(2, z), at(2, z) + cut]

    gathered, starts = [], []
    for blocks, piece in zip(lists, reduced, strict=True):
        other = send(piece, SWAP)
        gathered.append(ring(piece) + ring(other))
        starts.append(jnp.stack(places(blocks, half) + places(blocks, 1 - half)).astype(jnp.int32))

    rim_y = jax.ShapeDtypeStruct((tile_x, RIM, depth_cells), jnp.float32)
    rim_x = jax.ShapeDtypeStruct((RIM,) + s.shape[1:], jnp.float32)
    n = len(gathered[0])
    g, low, high = pl.pallas_call(
        functools.partial(frame_kernel, n),
        out_shape=(wide, rim_y, rim_y),
        in_specs=smem(3) + vmem(n + 1),
        out_specs=vmem(3),
        compiler_params=big,
        name="frame",
    )(starts[0], *tables(lists[0]), *gathered[0], masked)
    before, after = halo(low, high, "line")
    g, low, high = pl.pallas_call(
        rim_kernel,
        out_shape=(wide, rim_x, rim_x),
        in_specs=vmem(3),
        out_specs=vmem(3),
        compiler_params=big,
        name="rims",
    )(g, before, after)
    low, high = halo(low, high, "profile")
    return pl.pallas_call(
        functools.partial(smooth_kernel, n),
        out_shape=tile,
        in_specs=smem(3) + vmem(n + 7),
        out_specs=pl.BlockSpec(memory_space=pltpu.VMEM),
        scratch_shapes=[pltpu.VMEM(s.shape, jnp.float32)] * 2,
        compiler_params=big,
        name="smooth",
    )(starts[1], *tables(lists[1]), *gathered[1], masked, s, a, t, low, high, g)


def solution(mesh):
    placed = (
        P("source", None, "profile", "line", None),
        P("source", None, "profile", "line", None),
        P("profile", "line", None),
        P("profile", "line"),
        P(),
        P(),
    )
    return jax.shard_map(
        shards, mesh=mesh, in_specs=placed, out_specs=P("profile", "line", None), check_vma=False
    )
```

```python
import functools

import jax
import jax.numpy as jnp
import numpy as np
from jax import lax
from jax.experimental import pallas as pl
from jax.experimental.pallas import tpu as pltpu
from jax.sharding import PartitionSpec as P

smoothing_rate = 0.15
support_width = 0.3
floor_eps = 1e-06
mark_radius = 3
ROWS = 16
RIM = 2
PAD = 8

UP = [(4 * z + y, 4 * z + (y + 1) % 4) for z in range(2) for y in range(4)]
DOWN = [(j, i) for i, j in UP]
ACROSS = [(4 * z + y, 4 * z + (y + 2) % 4) for z in range(2) for y in range(4)]
SWAP = [(4 * z + y, 4 * (1 - z) + y) for z in range(2) for y in range(4)]


def send(x, pairs):
    return lax.ppermute(x, "source", pairs)


def block_lists(tile_x, tile_y):
    groups = tile_y // ROWS
    every = [(p, g) for p in range(tile_x) for g in range(groups)]
    inner = [(p, g) for p, g in every if 4 <= p < tile_x - 4 and 0 < g < groups - 1]
    outer = [b for b in every if b not in inner]
    cut = len(outer) // 32 * 16
    return [outer[:cut], outer[cut:], inner]


def tables(blocks):
    arr = np.array(blocks, np.int32)
    return jnp.asarray(arr[:, 0]), jnp.asarray(arr[:, 1])


big = pltpu.CompilerParams(vmem_limit_bytes=11 * 2**20)


def hold(*arrays):
    return [pltpu.with_memory_space_constraint(x, pltpu.VMEM) for x in arrays]


def held(shape):
    return pltpu.VMEM(shape, jnp.float32)


def vmem(n):
    return [pl.BlockSpec(memory_space=pltpu.VMEM)] * n


def smem(n):
    return [pl.BlockSpec(memory_space=pltpu.SMEM)] * n


def partials(source_grad, adjoint_grad, planes, groups, starts, count):
    depth = source_grad.shape[-1]
    n = len(starts)
    width = depth // 2 if depth % 256 == 0 else depth

    def body(start_ref, plane_ref, group_ref, f_hbm, b_hbm, *refs):
        outs, (f_ref, b_ref, sems) = refs[: n // 2], refs[n // 2 :]

        def copies(k, i):
            at = start_ref[k] + i
            p = plane_ref[at]
            rows = pl.ds(pl.multiple_of(group_ref[at] * ROWS, ROWS), ROWS)
            j = k * count + i
            return [
                pltpu.make_async_copy(hbm.at[0, :, p, rows], ref.at[j], sems.at[m, j])
                for m, (hbm, ref) in enumerate([(f_hbm, f_ref), (b_hbm, b_ref)])
            ]

        for k in range(n):

            def begin(i, _, k=k):
                for c in copies(k, i):
                    c.start()
                return 0

            lax.fori_loop(0, count, begin, 0)
        for k in range(n):

            def one(i, _, k=k):
                for c in copies(k, i):
                    c.wait()
                j = k * count + i
                for lo in range(0, depth, width):
                    f = f_ref[j, :, :, lo : lo + width].astype(jnp.float32)
                    b = b_ref[j, :, :, lo : lo + width].astype(jnp.float32)
                    outs[k // 2][k % 2, 0, i, :, lo : lo + width] = f[0] * b[0] + f[1] * b[1] + f[2] * b[2]
                    outs[k // 2][k % 2, 1, i, :, lo : lo + width] = (f[0] * f[0] + f[1] * f[1] + f[2] * f[2]) * (
                        b[0] * b[0] + b[1] * b[1] + b[2] * b[2]
                    )
                return 0

            lax.fori_loop(0, count, one, 0)

    return pl.pallas_call(
        body,
        out_shape=[held((2, 2, count, ROWS, depth))] * (n // 2),
        in_specs=smem(3) + [pl.BlockSpec(memory_space=pl.ANY)] * 2,
        out_specs=vmem(n // 2),
        scratch_shapes=[pltpu.VMEM((n * count, 3, ROWS, depth), jnp.bfloat16)] * 2
        + [pltpu.SemaphoreType.DMA((2, n * count))],
        compiler_params=big,
        name="partials",
    )(jnp.stack(starts).astype(jnp.int32), planes, groups, *[pltpu.with_memory_space_constraint(x, pltpu.HBM) for x in (source_grad, adjoint_grad)])


def place(pieces, segments, starts_ref, plane_ref, group_ref, ms_ref, g_ref, rim, pad):
    for k, (piece, offset, count) in enumerate(segments):
        for i in range(count):
            at = starts_ref[k] + i
            p, g = plane_ref[at], group_ref[at]
            rows = pl.multiple_of(g * ROWS, ROWS)
            g_ref[p + rim, pl.ds(pl.multiple_of(pad + rows, 8), ROWS), :] = (
                pieces[piece][offset + i] * ms_ref[p, pl.ds(rows, ROWS), :]
            )


def frame_kernel(n, segments, starts, planes, groups, *refs):
    pieces, (ms, g, low, high) = refs[:n], refs[n:]
    place(pieces, segments, starts, planes, groups, ms, g, 0, 0)
    rows = ms.shape[1]

    def rim(p, _):
        low[p] = g[p, :RIM]
        high[p] = g[p, rows - RIM :]
        return 0

    lax.fori_loop(0, ms.shape[0], rim, 0)


def rim_kernel(tile, before, after, wide, low, high):
    planes, rows, depth = tile.shape
    zero = jnp.zeros((PAD, depth), jnp.float32)

    def fill(p, _):
        at = p + RIM
        wide[at, :PAD] = zero
        wide[at, PAD + rows :] = zero
        wide[at, PAD : PAD + rows] = tile[p]
        wide[at, PAD - RIM : PAD] = before[p]
        wide[at, PAD + rows : PAD + rows + RIM] = after[p]
        return 0

    lax.fori_loop(0, planes, fill, 0)
    low[...] = wide[RIM : 2 * RIM]
    high[...] = wide[planes : planes + RIM]


def neighbours(ref, p, r, n):
    here = ref[p, r : r + n]
    depth = here.shape[1]
    lane = lax.broadcasted_iota(jnp.int32, here.shape, 1)
    total = ref[p + 1, r : r + n] + ref[p - 1, r : r + n]
    total = total + (ref[p, r + 1 : r + n + 1] if r + n < ref.shape[1] else pltpu.roll(here, n - 1, 0))
    total = total + (ref[p, r - 1 : r + n - 1] if r else pltpu.roll(here, 1, 0))
    total = total + jnp.where(lane == depth - 1, 0.0, pltpu.roll(here, depth - 1, 1))
    total = total + jnp.where(lane == 0, 0.0, pltpu.roll(here, 1, 1))
    return here, total


def chunks(rows):
    return [(r, ROWS) for r in range(PAD, PAD + rows, ROWS)]


def assemble(wide, low, high, full):
    count = wide.shape[0] - 2 * RIM

    def copy(p, _):
        full[p + RIM] = wide[p + RIM]
        return 0

    lax.fori_loop(0, count, copy, 0)
    full[:RIM] = low[...]
    full[count + RIM :] = high[...]


def coefficient_kernel(wide, low, high, s, a, t):
    planes, rows = t.shape[:2]
    assemble(wide, low, high, s)

    def one(p, _):
        for r, n in [(0, PAD), *chunks(rows), (PAD + rows, PAD)]:
            here, total = neighbours(s, p, r, n)
            a[p, r : r + n] = 1.0 - smoothing_rate * here * total
        return 0

    lax.fori_loop(1, planes + 2 * RIM - 1, one, 0)

    def two(p, _):
        for r, n in chunks(rows):
            here = s[p + RIM, r : r + n]
            value = a[p + RIM, r : r + n]
            t[p, r - PAD : r - PAD + n] = jnp.where(here > 0.0, value / jnp.where(here > 0.0, here, 1.0), 0.0)
        return 0

    lax.fori_loop(0, planes, two, 0)


GROUPS = 4


def smooth_kernel(n, segments, starts, planes, groups, *refs):
    pieces, refs = refs[:n], refs[n:]
    low, high, wide, ms_hbm, s_hbm, a_hbm, t_hbm, out_hbm, g, g1, ms, s, a, t, out, sems = refs
    count, rows = out.shape[:2]
    framed, step = g.shape[0] // GROUPS, count // GROUPS
    ms_copy = pltpu.make_async_copy(ms_hbm, ms, sems.at[0, 0])
    ms_copy.start()
    arrivals = []
    for k in range(GROUPS):
        part = pl.ds(k * framed, framed)
        arrivals.append(
            [
                pltpu.make_async_copy(s_hbm.at[part], s.at[part], sems.at[1, k]),
                pltpu.make_async_copy(a_hbm.at[part], a.at[part], sems.at[2, k]),
            ]
        )
    t_copies = []
    for k in range(GROUPS):
        part = pl.ds(k * step, step)
        t_copies.append(pltpu.make_async_copy(t_hbm.at[part], t.at[part], sems.at[3, k]))
    for c in arrivals[0]:
        c.start()
    assemble(wide, low, high, g)
    ms_copy.wait()
    for c in sum(arrivals[1:], []) + t_copies:
        c.start()
    place(pieces, segments, starts, planes, groups, ms, g, RIM, PAD)

    def first(p, _):
        for r, m in [(0, PAD), *chunks(rows), (PAD + rows, PAD)]:
            here, total = neighbours(g, p, r, m)
            w = s[p, r : r + m]
            g1[p, r : r + m] = a[p, r : r + m] * here + smoothing_rate * w * w * total
        return 0

    for k in range(GROUPS):
        for c in arrivals[k]:
            c.wait()
        lax.fori_loop(max(1, k * framed), min(g.shape[0] - 1, (k + 1) * framed), first, 0)

    def second(p, _):
        for r, m in chunks(rows):
            here, total = neighbours(g1, p + RIM, r, m)
            out[p, r - PAD : r - PAD + m] = (
                t[p, r - PAD : r - PAD + m] * here + smoothing_rate * s[p + RIM, r : r + m] * total
            )
        return 0

    leaving = []
    for k in range(GROUPS):
        t_copies[k].wait()
        lax.fori_loop(k * step, (k + 1) * step, second, 0)
        part = pl.ds(k * step, step)
        leaving.append(pltpu.make_async_copy(out.at[part], out_hbm.at[part], sems.at[4, k]))
        leaving[-1].start()
    for c in leaving:
        c.wait()


def halo(low, high, axis):
    size = lax.axis_size(axis)
    up = [(i, i + 1) for i in range(size - 1)]
    return lax.ppermute(high, axis, up), lax.ppermute(low, axis, [(j, i) for i, j in up])


def with_rims(tile, before, after):
    planes, rows, depth = tile.shape
    rim = held((RIM, rows + 2 * PAD, depth))
    return pl.pallas_call(
        rim_kernel,
        out_shape=(held((planes + 2 * RIM, rows + 2 * PAD, depth)), rim, rim),
        in_specs=vmem(3),
        out_specs=vmem(3),
        compiler_params=big,
        name="rims",
    )(*hold(tile, before, after))


def shards(source_grad, adjoint_grad, log_model, surface_depth, source_columns, receiver_columns):
    tile_x, tile_y, depth_cells = log_model.shape
    me = lax.axis_index("source")
    y, half = me % 4, me // 4
    lists = block_lists(tile_x, tile_y)
    planes, groups = tables(sum(lists, []))
    parts = [len(blocks) // 8 for blocks in lists]
    after_rest = lax.optimization_barrier

    def start_of(k, offset, z):
        return 8 * sum(parts[:k]) + (2 * ((y + offset) % 4) + z) * parts[k]

    def sums_of(k):
        at = functools.partial(start_of, k)
        starts = [at(2, 1), at(1, 0), at(2, 0), at(-1, 1), at(-1, 0), at(1, 1), at(0, 0), at(0, 1)]
        return partials(source_grad, adjoint_grad, planes, groups, starts, parts[k])

    def first_step(up, down):
        return send(up, UP), send(down, DOWN)

    def second_step(up, down, keep):
        return keep[0] + down[0], keep[1] + up[0]

    def finish(own, up, down, end0, end1):
        own0 = own[0] + up[1] + end0
        own1 = own[1] + down[1] + end1
        return jnp.where(half == 0, own0, own1), jnp.where(half == 0, own1, own0)

    def normalised(own, other):
        total = own + other
        return total[0] * lax.rsqrt(total[1] + floor_eps)

    def ring(piece):
        return [piece, send(piece, UP), send(piece, DOWN), send(piece, ACROSS)]

    ring_offsets = (0, -1, 1, 2)

    up, down, keep, own = sums_of(0)
    log_model, up = after_rest((log_model, up))
    up, down = first_step(up, down)
    depth_index = lax.broadcasted_iota(jnp.int32, (tile_x, tile_y, depth_cells), 2)
    total_y = tile_y * lax.axis_size("line")
    columns = jnp.concatenate([source_columns, receiver_columns])
    electrode_x = columns // total_y
    electrode_y = columns % total_y
    global_x = lax.broadcasted_iota(jnp.int32, (1, tile_x), 1) + lax.axis_index("profile") * tile_x
    global_y = lax.broadcasted_iota(jnp.int32, (1, tile_y), 1) + lax.axis_index("line") * tile_y
    near_x = (jnp.abs(global_x - electrode_x[:, None]) <= mark_radius).astype(jnp.float32)
    near_y = (jnp.abs(global_y - electrode_y[:, None]) <= mark_radius).astype(jnp.float32)
    covered = jnp.einsum("ex,ey->xy", near_x, near_y, precision=lax.Precision.HIGHEST)
    threshold = surface_depth + jnp.where(covered > 0.5, depth_cells // 16, 0)
    root = support_width * lax.rsqrt(log_model * log_model + support_width * support_width)
    root = jnp.where(depth_index >= surface_depth[:, :, None], root, 0.0)
    masked = jnp.where(depth_index >= threshold[:, :, None], root, 0.0)
    up, down, root, masked = after_rest((up, down, root, masked))
    end0, end1 = second_step(up, down, keep)
    source_grad, adjoint_grad, end0, end1 = after_rest((source_grad, adjoint_grad, end0, end1))
    end0, end1 = send(end0, DOWN), send(end1, UP)

    up2, down2, keep2, own2 = sums_of(1)
    before, after = halo(root[:, :RIM], root[:, -RIM:], "line")
    own, leaving = finish(own, up, down, end0, end1)
    up2, down2, leaving, root = after_rest((up2, down2, leaving, root))
    other = send(leaving, SWAP)
    up, down = first_step(up2, down2)
    wide, low, high = with_rims(root, before, after)
    low, high = halo(low, high, "profile")
    up, down, wide, low, high = after_rest((up, down, wide, low, high))
    end0, end1 = second_step(up, down, keep2)
    source_grad, adjoint_grad, end0, end1, other = after_rest((source_grad, adjoint_grad, end0, end1, other))
    end0, end1 = send(end0, DOWN), send(end1, UP)

    up3, down3, keep3, own3 = sums_of(2)
    own2, leaving = finish(own2, up, down, end0, end1)
    up3, down3, leaving, wide = after_rest((up3, down3, leaving, wide))
    other2 = send(leaving, SWAP)
    up, down = first_step(up3, down3)
    s, a, t = pl.pallas_call(
        coefficient_kernel,
        out_shape=(held(wide.shape),) * 2 + (held(log_model.shape),),
        in_specs=vmem(3),
        out_specs=vmem(3),
        compiler_params=big,
        name="coefficients",
    )(*hold(wide, low, high))
    up, down, s, a, t, other2 = after_rest((up, down, s, a, t, other2))
    end0, end1 = second_step(up, down, keep3)
    end0, end1 = send(end0, DOWN), send(end1, UP)
    frame = jnp.concatenate([normalised(own, other), normalised(own2, other2)])
    frame_other = send(frame, SWAP)
    frame_ring = ring(frame)
    own3, leaving = finish(own3, up, down, end0, end1)
    inner = normalised(own3, send(leaving, SWAP))
    inner_other = send(inner, SWAP)
    other_ring = ring(frame_other)
    inner_rings = ring(inner) + ring(inner_other)
    frame_ring, other_ring, inner_other = after_rest((frame_ring, other_ring, inner_other))

    def segments_of(ranges):
        segments = [(i, offset, parts[k]) for i, piece in enumerate(ranges) for k, _, offset, _ in piece]
        starts = jnp.stack([start_of(k, q, z) for piece in ranges for k, z, _, q in piece])
        return segments, starts.astype(jnp.int32)

    pieces = frame_ring + other_ring
    segments, starts = segments_of([[(0, z, 0, q), (1, z, parts[0], q)] for z in (half, 1 - half) for q in ring_offsets])
    rim_y = held((tile_x, RIM, depth_cells))
    g, low, high = pl.pallas_call(
        functools.partial(frame_kernel, len(pieces), segments),
        out_shape=(held(log_model.shape), rim_y, rim_y),
        in_specs=smem(3) + vmem(len(pieces) + 1),
        out_specs=vmem(3),
        compiler_params=big,
        name="frame",
    )(starts, planes, groups, *hold(*pieces, masked))
    before, after = halo(low, high, "line")
    before, after, inner_rings = after_rest((before, after, inner_rings))
    g, low, high = with_rims(g, before, after)
    low, high = halo(low, high, "profile")
    pieces = inner_rings
    segments, starts = segments_of(
        [[(2, z, 0, q)] for z in (half, 1 - half) for q in ring_offsets]
    )
    wide_f32, tile_f32 = pltpu.VMEM(s.shape, jnp.float32), pltpu.VMEM(log_model.shape, jnp.float32)
    anywhere = pl.BlockSpec(memory_space=pl.ANY)
    return pl.pallas_call(
        functools.partial(smooth_kernel, len(pieces), segments),
        out_shape=jax.ShapeDtypeStruct(log_model.shape, jnp.float32),
        in_specs=smem(3) + vmem(len(pieces) + 3) + [anywhere] * 4,
        out_specs=anywhere,
        scratch_shapes=[wide_f32, wide_f32, tile_f32, wide_f32, wide_f32, tile_f32, tile_f32]
        + [pltpu.SemaphoreType.DMA((5, GROUPS))],
        compiler_params=pltpu.CompilerParams(vmem_limit_bytes=40 * 2**20),
        name="smooth",
    )(starts, planes, groups, *hold(*pieces, low, high, g), masked, s, a, t)


def solution(mesh):
    placed = (
        P("source", None, "profile", "line", None),
        P("source", None, "profile", "line", None),
        P("profile", "line", None),
        P("profile", "line"),
        P(),
        P(),
    )
    return jax.shard_map(
        shards, mesh=mesh, in_specs=placed, out_specs=P("profile", "line", None), check_vma=False
    )
```

```python
import functools

import jax
import jax.numpy as jnp
import numpy as np
from jax import lax
from jax.experimental import pallas as pl
from jax.experimental.pallas import tpu as pltpu
from jax.sharding import PartitionSpec as P

smoothing_rate = 0.15
support_width = 0.3
floor_eps = 1e-06
mark_radius = 3
ROWS = 16
RIM = 2
PAD = 8

UP = [(4 * z + y, 4 * z + (y + 1) % 4) for z in range(2) for y in range(4)]
DOWN = [(j, i) for i, j in UP]
ACROSS = [(4 * z + y, 4 * z + (y + 2) % 4) for z in range(2) for y in range(4)]
SWAP = [(4 * z + y, 4 * (1 - z) + y) for z in range(2) for y in range(4)]


def send(x, pairs):
    return lax.ppermute(x, "source", pairs)


def block_lists(tile_x, tile_y):
    groups = tile_y // ROWS
    every = [(p, g) for p in range(tile_x) for g in range(groups)]
    inner = [(p, g) for p, g in every if 4 <= p < tile_x - 4 and 0 < g < groups - 1]
    outer = [b for b in every if b not in inner]
    cut = len(outer) // 32 * 16
    return [outer[:cut], outer[cut:], inner]


def tables(blocks):
    arr = np.array(blocks, np.int32)
    return jnp.asarray(arr[:, 0]), jnp.asarray(arr[:, 1])


big = pltpu.CompilerParams(vmem_limit_bytes=11 * 2**20)


def hold(*arrays):
    return [pltpu.with_memory_space_constraint(x, pltpu.VMEM) for x in arrays]


def in_hbm(*arrays):
    return [pltpu.with_memory_space_constraint(x, pltpu.HBM) for x in arrays]


def held(shape):
    return pltpu.VMEM(shape, jnp.float32)


def vmem(n):
    return [pl.BlockSpec(memory_space=pltpu.VMEM)] * n


def smem(n):
    return [pl.BlockSpec(memory_space=pltpu.SMEM)] * n


def partials(source_grad, adjoint_grad, planes, groups, starts, count):
    depth = source_grad.shape[-1]
    n = len(starts)
    width = depth // 2 if depth % 256 == 0 else depth

    def body(start_ref, plane_ref, group_ref, f_hbm, b_hbm, *refs):
        outs, (f_ref, b_ref, sems) = refs[: n // 2], refs[n // 2 :]

        def copies(k, i):
            at = start_ref[k] + i
            p = plane_ref[at]
            rows = pl.ds(pl.multiple_of(group_ref[at] * ROWS, ROWS), ROWS)
            j = k * count + i
            return [
                pltpu.make_async_copy(hbm.at[0, :, p, rows], ref.at[j], sems.at[m, j])
                for m, (hbm, ref) in enumerate([(f_hbm, f_ref), (b_hbm, b_ref)])
            ]

        for k in range(n):

            def begin(i, _, k=k):
                for c in copies(k, i):
                    c.start()
                return 0

            lax.fori_loop(0, count, begin, 0)
        for k in range(n):

            def one(i, _, k=k):
                for c in copies(k, i):
                    c.wait()
                j = k * count + i
                for lo in range(0, depth, width):
                    f = f_ref[j, :, :, lo : lo + width].astype(jnp.float32)
                    b = b_ref[j, :, :, lo : lo + width].astype(jnp.float32)
                    outs[k // 2][k % 2, 0, i, :, lo : lo + width] = f[0] * b[0] + f[1] * b[1] + f[2] * b[2]
                    outs[k // 2][k % 2, 1, i, :, lo : lo + width] = (f[0] * f[0] + f[1] * f[1] + f[2] * f[2]) * (
                        b[0] * b[0] + b[1] * b[1] + b[2] * b[2]
                    )
                return 0

            lax.fori_loop(0, count, one, 0)

    return pl.pallas_call(
        body,
        out_shape=[held((2, 2, count, ROWS, depth))] * (n // 2),
        in_specs=smem(3) + [pl.BlockSpec(memory_space=pl.ANY)] * 2,
        out_specs=vmem(n // 2),
        scratch_shapes=[pltpu.VMEM((n * count, 3, ROWS, depth), jnp.bfloat16)] * 2
        + [pltpu.SemaphoreType.DMA((2, n * count))],
        compiler_params=big,
        name="partials",
    )(jnp.stack(starts).astype(jnp.int32), planes, groups, *in_hbm(source_grad, adjoint_grad))


def place(pieces, segments, starts_ref, plane_ref, group_ref, ms_ref, g_ref, rim, pad):
    for k, (piece, offset, count) in enumerate(segments):
        for i in range(count):
            at = starts_ref[k] + i
            p, g = plane_ref[at], group_ref[at]
            rows = pl.multiple_of(g * ROWS, ROWS)
            g_ref[p + rim, pl.ds(pl.multiple_of(pad + rows, 8), ROWS), :] = (
                pieces[piece][offset + i] * ms_ref[p, pl.ds(rows, ROWS), :]
            )


def frame_kernel(n, segments, starts, planes, groups, *refs):
    pieces, (ms, g, low, high, first, last) = refs[:n], refs[n:]
    place(pieces, segments, starts, planes, groups, ms, g, 0, 0)
    rows = ms.shape[1]

    def rim(p, _):
        low[p] = g[p, :RIM]
        high[p] = g[p, rows - RIM :]
        return 0

    lax.fori_loop(0, ms.shape[0], rim, 0)
    first[...] = g[:RIM]
    last[...] = g[ms.shape[0] - RIM :]


def corner_kernel(first, last, before, after, low, high):
    planes, rows, depth = first.shape
    zero = jnp.zeros((PAD, depth), jnp.float32)
    for tile, out, at in ((first, low, 0), (last, high, before.shape[0] - RIM)):
        for p in range(planes):
            out[p, :PAD] = zero
            out[p, PAD + rows :] = zero
            out[p, PAD : PAD + rows] = tile[p]
            out[p, PAD - RIM : PAD] = before[at + p]
            out[p, PAD + rows : PAD + rows + RIM] = after[at + p]


def rim_kernel(tile, before, after, wide, low, high):
    planes, rows, depth = tile.shape
    zero = jnp.zeros((PAD, depth), jnp.float32)

    def fill(p, _):
        at = p + RIM
        wide[at, :PAD] = zero
        wide[at, PAD + rows :] = zero
        wide[at, PAD : PAD + rows] = tile[p]
        wide[at, PAD - RIM : PAD] = before[p]
        wide[at, PAD + rows : PAD + rows + RIM] = after[p]
        return 0

    lax.fori_loop(0, planes, fill, 0)
    low[...] = wide[RIM : 2 * RIM]
    high[...] = wide[planes : planes + RIM]


def neighbours(ref, p, r, n):
    here = ref[p, r : r + n]
    depth = here.shape[1]
    lane = lax.broadcasted_iota(jnp.int32, here.shape, 1)
    total = ref[p + 1, r : r + n] + ref[p - 1, r : r + n]
    total = total + (ref[p, r + 1 : r + n + 1] if r + n < ref.shape[1] else pltpu.roll(here, n - 1, 0))
    total = total + (ref[p, r - 1 : r + n - 1] if r else pltpu.roll(here, 1, 0))
    total = total + jnp.where(lane == depth - 1, 0.0, pltpu.roll(here, depth - 1, 1))
    total = total + jnp.where(lane == 0, 0.0, pltpu.roll(here, 1, 1))
    return here, total


def chunks(rows):
    return [(r, ROWS) for r in range(PAD, PAD + rows, ROWS)]


def assemble(wide, low, high, full):
    count = wide.shape[0] - 2 * RIM

    def copy(p, _):
        full[p + RIM] = wide[p + RIM]
        return 0

    lax.fori_loop(0, count, copy, 0)
    full[:RIM] = low[...]
    full[count + RIM :] = high[...]


def coefficient_kernel(wide, low, high, s, a, t):
    planes, rows = t.shape[:2]
    assemble(wide, low, high, s)

    def one(p, _):
        for r, n in [(0, PAD), *chunks(rows), (PAD + rows, PAD)]:
            here, total = neighbours(s, p, r, n)
            a[p, r : r + n] = 1.0 - smoothing_rate * here * total
        return 0

    lax.fori_loop(1, planes + 2 * RIM - 1, one, 0)

    def two(p, _):
        for r, n in chunks(rows):
            here = s[p + RIM, r : r + n]
            value = a[p + RIM, r : r + n]
            t[p, r - PAD : r - PAD + n] = jnp.where(here > 0.0, value / jnp.where(here > 0.0, here, 1.0), 0.0)
        return 0

    lax.fori_loop(0, planes, two, 0)


GROUPS = 4


def smooth_kernel(n, segments, starts, planes, groups, *refs):
    pieces, refs = refs[:n], refs[n:]
    low, high, before, after, ms_hbm, tile_hbm, s_hbm, a_hbm, t_hbm, out_hbm, g, g1, s, a, t, sems = refs
    count, rows = t.shape[:2]
    ms = g1.at[pl.ds(0, count), pl.ds(0, rows)]
    framed, step = g.shape[0] // GROUPS, count // GROUPS
    ms_copy = pltpu.make_async_copy(ms_hbm, ms, sems.at[0, 0])
    inside = g.at[pl.ds(RIM, count), pl.ds(PAD, rows)]
    g_copy = pltpu.make_async_copy(tile_hbm, inside, sems.at[0, 1])
    ms_copy.start()
    g_copy.start()
    arrivals = []
    for k in range(GROUPS):
        part = pl.ds(k * framed, framed)
        arrivals.append(
            [
                pltpu.make_async_copy(s_hbm.at[part], s.at[part], sems.at[1, k]),
                pltpu.make_async_copy(a_hbm.at[part], a.at[part], sems.at[2, k]),
            ]
        )
    t_copies = []
    for k in range(GROUPS):
        part = pl.ds(k * step, step)
        t_copies.append(pltpu.make_async_copy(t_hbm.at[part], t.at[part], sems.at[3, k]))
    for c in arrivals[0]:
        c.start()
    g[:RIM] = low[...]
    g[count + RIM :] = high[...]
    zero = jnp.zeros((PAD, g.shape[2]), jnp.float32)

    def rims(p, _):
        at = p + RIM
        g[at, :PAD] = zero
        g[at, PAD + rows :] = zero
        g[at, PAD - RIM : PAD] = before[p]
        g[at, PAD + rows : PAD + rows + RIM] = after[p]
        return 0

    lax.fori_loop(0, count, rims, 0)
    ms_copy.wait()
    g_copy.wait()
    for c in sum(arrivals[1:], []) + t_copies:
        c.start()
    place(pieces, segments, starts, planes, groups, ms, g, RIM, PAD)

    def first(p, _):
        for r, m in [(0, PAD), *chunks(rows), (PAD + rows, PAD)]:
            here, total = neighbours(g, p, r, m)
            w = s[p, r : r + m]
            g1[p, r : r + m] = a[p, r : r + m] * here + smoothing_rate * w * w * total
        return 0

    for k in range(GROUPS):
        for c in arrivals[k]:
            c.wait()
        lax.fori_loop(max(1, k * framed), min(g.shape[0] - 1, (k + 1) * framed), first, 0)

    def second(p, _):
        for r, m in chunks(rows):
            here, total = neighbours(g1, p + RIM, r, m)
            t[p, r - PAD : r - PAD + m] = (
                t[p, r - PAD : r - PAD + m] * here + smoothing_rate * s[p + RIM, r : r + m] * total
            )
        return 0

    leaving = []
    for k in range(GROUPS):
        t_copies[k].wait()
        lax.fori_loop(k * step, (k + 1) * step, second, 0)
        part = pl.ds(k * step, step)
        leaving.append(pltpu.make_async_copy(t.at[part], out_hbm.at[part], sems.at[4, k]))
        leaving[-1].start()
    for c in leaving:
        c.wait()


def halo(low, high, axis):
    size = lax.axis_size(axis)
    up = [(i, i + 1) for i in range(size - 1)]
    return lax.ppermute(high, axis, up), lax.ppermute(low, axis, [(j, i) for i, j in up])


def with_rims(tile, before, after):
    planes, rows, depth = tile.shape
    rim = held((RIM, rows + 2 * PAD, depth))
    return pl.pallas_call(
        rim_kernel,
        out_shape=(held((planes + 2 * RIM, rows + 2 * PAD, depth)), rim, rim),
        in_specs=vmem(3),
        out_specs=vmem(3),
        compiler_params=big,
        name="rims",
    )(*hold(tile, before, after))


def shards(source_grad, adjoint_grad, log_model, surface_depth, source_columns, receiver_columns):
    tile_x, tile_y, depth_cells = log_model.shape
    me = lax.axis_index("source")
    y, half = me % 4, me // 4
    lists = block_lists(tile_x, tile_y)
    planes, groups = tables(sum(lists, []))
    parts = [len(blocks) // 8 for blocks in lists]
    after_rest = lax.optimization_barrier

    def start_of(k, offset, z):
        return 8 * sum(parts[:k]) + (2 * ((y + offset) % 4) + z) * parts[k]

    def sums_of(k):
        at = functools.partial(start_of, k)
        starts = [at(2, 1), at(1, 0), at(2, 0), at(-1, 1), at(-1, 0), at(1, 1), at(0, 0), at(0, 1)]
        return partials(source_grad, adjoint_grad, planes, groups, starts, parts[k])

    def first_step(up, down):
        return send(up, UP), send(down, DOWN)

    def second_step(up, down, keep):
        return keep[0] + down[0], keep[1] + up[0]

    def finish(own, up, down, end0, end1):
        own0 = own[0] + up[1] + end0
        own1 = own[1] + down[1] + end1
        return jnp.where(half == 0, own0, own1), jnp.where(half == 0, own1, own0)

    def normalised(own, other):
        total = own + other
        return total[0] * lax.rsqrt(total[1] + floor_eps)

    def ring(piece):
        return [piece, send(piece, UP), send(piece, DOWN), send(piece, ACROSS)]

    ring_offsets = (0, -1, 1, 2)

    up, down, keep, own = sums_of(0)
    log_model, up = after_rest((log_model, up))
    up, down = first_step(up, down)
    depth_index = lax.broadcasted_iota(jnp.int32, (tile_x, tile_y, depth_cells), 2)
    total_y = tile_y * lax.axis_size("line")
    columns = jnp.concatenate([source_columns, receiver_columns])
    electrode_x = columns // total_y
    electrode_y = columns % total_y
    global_x = lax.broadcasted_iota(jnp.int32, (1, tile_x), 1) + lax.axis_index("profile") * tile_x
    global_y = lax.broadcasted_iota(jnp.int32, (1, tile_y), 1) + lax.axis_index("line") * tile_y
    near_x = (jnp.abs(global_x - electrode_x[:, None]) <= mark_radius).astype(jnp.float32)
    near_y = (jnp.abs(global_y - electrode_y[:, None]) <= mark_radius).astype(jnp.float32)
    covered = jnp.einsum("ex,ey->xy", near_x, near_y, precision=lax.Precision.HIGHEST)
    threshold = surface_depth + jnp.where(covered > 0.5, depth_cells // 16, 0)
    root = support_width * lax.rsqrt(log_model * log_model + support_width * support_width)
    root = jnp.where(depth_index >= surface_depth[:, :, None], root, 0.0)
    masked = jnp.where(depth_index >= threshold[:, :, None], root, 0.0)
    up, down, root, masked = after_rest((up, down, root, masked))
    end0, end1 = second_step(up, down, keep)
    source_grad, adjoint_grad, end0, end1 = after_rest((source_grad, adjoint_grad, end0, end1))
    end0, end1 = send(end0, DOWN), send(end1, UP)

    up2, down2, keep2, own2 = sums_of(1)
    own, leaving = finish(own, up, down, end0, end1)
    up2, down2, leaving = after_rest((up2, down2, leaving))
    other = send(leaving, SWAP)
    up, down = first_step(up2, down2)
    end0, end1 = second_step(up, down, keep2)
    source_grad, adjoint_grad, end0, end1, other = after_rest((source_grad, adjoint_grad, end0, end1, other))
    end0, end1 = send(end0, DOWN), send(end1, UP)

    up3, down3, keep3, own3 = sums_of(2)
    own2, leaving = finish(own2, up, down, end0, end1)
    up3, down3, leaving, root = after_rest((up3, down3, leaving, root))
    other2 = send(leaving, SWAP)
    up, down = first_step(up3, down3)
    before, after = halo(root[:, :RIM], root[:, -RIM:], "line")
    wide, low, high = with_rims(root, before, after)
    low, high = halo(low, high, "profile")
    s, a, t = pl.pallas_call(
        coefficient_kernel,
        out_shape=(held(wide.shape),) * 2 + (held(log_model.shape),),
        in_specs=vmem(3),
        out_specs=vmem(3),
        compiler_params=big,
        name="coefficients",
    )(*hold(wide, low, high))
    up, down, wide, other2 = after_rest((up, down, wide, other2))
    end0, end1 = second_step(up, down, keep3)
    end0, end1 = send(end0, DOWN), send(end1, UP)
    frame = jnp.concatenate([normalised(own, other), normalised(own2, other2)])
    frame_other = send(frame, SWAP)
    frame_ring = ring(frame)
    end0, end1, frame_other, s, a, t = after_rest((end0, end1, frame_other, s, a, t))
    own3, leaving = finish(own3, up, down, end0, end1)
    inner = normalised(own3, send(leaving, SWAP))
    inner_other = send(inner, SWAP)
    other_ring = ring(frame_other)
    inner_rings = ring(inner) + ring(inner_other)

    def segments_of(ranges):
        segments = [(i, offset, parts[k]) for i, piece in enumerate(ranges) for k, _, offset, _ in piece]
        starts = jnp.stack([start_of(k, q, z) for piece in ranges for k, z, _, q in piece])
        return segments, starts.astype(jnp.int32)

    pieces = frame_ring + other_ring
    segments, starts = segments_of([[(0, z, 0, q), (1, z, parts[0], q)] for z in (half, 1 - half) for q in ring_offsets])
    rim_y, rim_x = held((tile_x, RIM, depth_cells)), held((RIM, tile_y, depth_cells))
    g, low, high, first, last = pl.pallas_call(
        functools.partial(frame_kernel, len(pieces), segments),
        out_shape=(jax.ShapeDtypeStruct(log_model.shape, jnp.float32), rim_y, rim_y, rim_x, rim_x),
        in_specs=smem(3) + vmem(len(pieces) + 1),
        out_specs=vmem(5),
        compiler_params=big,
        name="frame",
    )(starts, planes, groups, *hold(*pieces, masked))
    before, after = halo(low, high, "line")
    before, after, inner_rings = after_rest((before, after, inner_rings))
    low, high = pl.pallas_call(
        corner_kernel,
        out_shape=(held((RIM, tile_y + 2 * PAD, depth_cells)),) * 2,
        in_specs=vmem(4),
        out_specs=vmem(2),
        compiler_params=big,
        name="corners",
    )(*hold(first, last, before, after))
    low, high = halo(low, high, "profile")
    pieces = inner_rings
    segments, starts = segments_of(
        [[(2, z, 0, q)] for z in (half, 1 - half) for q in ring_offsets]
    )
    wide_f32, tile_f32 = pltpu.VMEM(s.shape, jnp.float32), pltpu.VMEM(log_model.shape, jnp.float32)
    anywhere = pl.BlockSpec(memory_space=pl.ANY)
    return pl.pallas_call(
        functools.partial(smooth_kernel, len(pieces), segments),
        out_shape=jax.ShapeDtypeStruct(log_model.shape, jnp.float32),
        in_specs=smem(3) + vmem(len(pieces) + 4) + [anywhere] * 5,
        out_specs=anywhere,
        scratch_shapes=[wide_f32, wide_f32, wide_f32, wide_f32, tile_f32]
        + [pltpu.SemaphoreType.DMA((5, GROUPS))],
        compiler_params=pltpu.CompilerParams(vmem_limit_bytes=30 * 2**20),
        name="smooth",
    )(starts, planes, groups, *hold(*pieces, low, high, before, after), *in_hbm(masked, g, s, a, t))


def solution(mesh):
    placed = (
        P("source", None, "profile", "line", None),
        P("source", None, "profile", "line", None),
        P("profile", "line", None),
        P("profile", "line"),
        P(),
        P(),
    )
    return jax.shard_map(
        shards, mesh=mesh, in_specs=placed, out_specs=P("profile", "line", None), check_vma=False
    )
```

```python
import functools

import jax
import jax.numpy as jnp
import numpy as np
from jax import lax
from jax.experimental import pallas as pl
from jax.experimental.pallas import tpu as pltpu
from jax.sharding import PartitionSpec as P

smoothing_rate = 0.15
support_width = 0.3
floor_eps = 1e-06
mark_radius = 3
ROWS = 16
RIM = 2
PAD = 8

UP = [(4 * z + y, 4 * z + (y + 1) % 4) for z in range(2) for y in range(4)]
DOWN = [(j, i) for i, j in UP]
ACROSS = [(4 * z + y, 4 * z + (y + 2) % 4) for z in range(2) for y in range(4)]
SWAP = [(4 * z + y, 4 * (1 - z) + y) for z in range(2) for y in range(4)]


def send(x, pairs):
    return lax.ppermute(x, "source", pairs)


def block_lists(tile_x, tile_y):
    groups = tile_y // ROWS
    every = [(p, g) for p in range(tile_x) for g in range(groups)]
    inner = [(p, g) for p, g in every if 4 <= p < tile_x - 4 and 0 < g < groups - 1]
    outer = [b for b in every if b not in inner]
    cut = len(outer) // 32 * 16
    return [outer[:cut], outer[cut:], inner]


def tables(blocks):
    arr = np.array(blocks, np.int32)
    return jnp.asarray(arr[:, 0]), jnp.asarray(arr[:, 1])


big = pltpu.CompilerParams(vmem_limit_bytes=11 * 2**20)


def hold(*arrays):
    return [pltpu.with_memory_space_constraint(x, pltpu.VMEM) for x in arrays]


def in_hbm(*arrays):
    return [pltpu.with_memory_space_constraint(x, pltpu.HBM) for x in arrays]


def held(shape):
    return pltpu.VMEM(shape, jnp.float32)


def vmem(n):
    return [pl.BlockSpec(memory_space=pltpu.VMEM)] * n


def smem(n):
    return [pl.BlockSpec(memory_space=pltpu.SMEM)] * n


def partials(source_grad, adjoint_grad, planes, groups, starts, count):
    depth = source_grad.shape[-1]
    n = len(starts)
    width = depth // 2 if depth % 256 == 0 else depth

    def body(start_ref, plane_ref, group_ref, f_hbm, b_hbm, *refs):
        outs, (f_ref, b_ref, sems) = refs[: n // 2], refs[n // 2 :]

        def copies(k, i):
            at = start_ref[k] + i
            p = plane_ref[at]
            rows = pl.ds(pl.multiple_of(group_ref[at] * ROWS, ROWS), ROWS)
            j = k * count + i
            return [
                pltpu.make_async_copy(hbm.at[0, :, p, rows], ref.at[j], sems.at[m, j])
                for m, (hbm, ref) in enumerate([(f_hbm, f_ref), (b_hbm, b_ref)])
            ]

        for k in range(n):

            def begin(i, _, k=k):
                for c in copies(k, i):
                    c.start()
                return 0

            lax.fori_loop(0, count, begin, 0)
        for k in range(n):

            def one(i, _, k=k):
                for c in copies(k, i):
                    c.wait()
                j = k * count + i
                for lo in range(0, depth, width):
                    f = f_ref[j, :, :, lo : lo + width].astype(jnp.float32)
                    b = b_ref[j, :, :, lo : lo + width].astype(jnp.float32)
                    outs[k // 2][k % 2, 0, i, :, lo : lo + width] = f[0] * b[0] + f[1] * b[1] + f[2] * b[2]
                    outs[k // 2][k % 2, 1, i, :, lo : lo + width] = (f[0] * f[0] + f[1] * f[1] + f[2] * f[2]) * (
                        b[0] * b[0] + b[1] * b[1] + b[2] * b[2]
                    )
                return 0

            lax.fori_loop(0, count, one, 0)

    return pl.pallas_call(
        body,
        out_shape=[held((2, 2, count, ROWS, depth))] * (n // 2),
        in_specs=smem(3) + [pl.BlockSpec(memory_space=pl.ANY)] * 2,
        out_specs=vmem(n // 2),
        scratch_shapes=[pltpu.VMEM((n * count, 3, ROWS, depth), jnp.bfloat16)] * 2
        + [pltpu.SemaphoreType.DMA((2, n * count))],
        compiler_params=big,
        name="partials",
    )(jnp.stack(starts).astype(jnp.int32), planes, groups, *in_hbm(source_grad, adjoint_grad))


def place(pieces, segments, starts_ref, plane_ref, group_ref, ms_ref, g_ref, rim, pad):
    for k, (piece, offset, count) in enumerate(segments):
        for i in range(count):
            at = starts_ref[k] + i
            p, g = plane_ref[at], group_ref[at]
            rows = pl.multiple_of(g * ROWS, ROWS)
            g_ref[p + rim, pl.ds(pl.multiple_of(pad + rows, 8), ROWS), :] = (
                pieces[piece][offset + i] * ms_ref[p, pl.ds(rows, ROWS), :]
            )


def frame_kernel(n, segments, starts, planes, groups, *refs):
    pieces, (ms, g, low, high, first, last) = refs[:n], refs[n:]
    place(pieces, segments, starts, planes, groups, ms, g, 0, 0)
    rows = ms.shape[1]

    def rim(p, _):
        low[p] = g[p, :RIM]
        high[p] = g[p, rows - RIM :]
        return 0

    lax.fori_loop(0, ms.shape[0], rim, 0)
    first[...] = g[:RIM]
    last[...] = g[ms.shape[0] - RIM :]


def corner_kernel(first, last, before, after, low, high):
    planes, rows, depth = first.shape
    zero = jnp.zeros((PAD, depth), jnp.float32)
    for tile, out, at in ((first, low, 0), (last, high, before.shape[0] - RIM)):
        for p in range(planes):
            out[p, :PAD] = zero
            out[p, PAD + rows :] = zero
            out[p, PAD : PAD + rows] = tile[p]
            out[p, PAD - RIM : PAD] = before[at + p]
            out[p, PAD + rows : PAD + rows + RIM] = after[at + p]


def rim_kernel(tile, before, after, wide, low, high):
    planes, rows, depth = tile.shape
    zero = jnp.zeros((PAD, depth), jnp.float32)

    def fill(p, _):
        at = p + RIM
        wide[at, :PAD] = zero
        wide[at, PAD + rows :] = zero
        wide[at, PAD : PAD + rows] = tile[p]
        wide[at, PAD - RIM : PAD] = before[p]
        wide[at, PAD + rows : PAD + rows + RIM] = after[p]
        return 0

    lax.fori_loop(0, planes, fill, 0)
    low[...] = wide[RIM : 2 * RIM]
    high[...] = wide[planes : planes + RIM]


def neighbours(ref, p, r, n):
    here = ref[p, r : r + n]
    depth = here.shape[1]
    lane = lax.broadcasted_iota(jnp.int32, here.shape, 1)
    total = ref[p + 1, r : r + n] + ref[p - 1, r : r + n]
    total = total + (ref[p, r + 1 : r + n + 1] if r + n < ref.shape[1] else pltpu.roll(here, n - 1, 0))
    total = total + (ref[p, r - 1 : r + n - 1] if r else pltpu.roll(here, 1, 0))
    total = total + jnp.where(lane == depth - 1, 0.0, pltpu.roll(here, depth - 1, 1))
    total = total + jnp.where(lane == 0, 0.0, pltpu.roll(here, 1, 1))
    return here, total


def chunks(rows):
    return [(r, ROWS) for r in range(PAD, PAD + rows, ROWS)]


def assemble(wide, low, high, full):
    count = wide.shape[0] - 2 * RIM

    def copy(p, _):
        full[p + RIM] = wide[p + RIM]
        return 0

    lax.fori_loop(0, count, copy, 0)
    full[:RIM] = low[...]
    full[count + RIM :] = high[...]


def coefficient_kernel(wide, low, high, s, a, t):
    planes, rows = t.shape[:2]
    assemble(wide, low, high, s)

    def one(p, _):
        for r, n in [(0, PAD), *chunks(rows), (PAD + rows, PAD)]:
            here, total = neighbours(s, p, r, n)
            a[p, r : r + n] = 1.0 - smoothing_rate * here * total
        return 0

    lax.fori_loop(1, planes + 2 * RIM - 1, one, 0)

    def two(p, _):
        for r, n in chunks(rows):
            here = s[p + RIM, r : r + n]
            value = a[p + RIM, r : r + n]
            t[p, r - PAD : r - PAD + n] = jnp.where(here > 0.0, value / jnp.where(here > 0.0, here, 1.0), 0.0)
        return 0

    lax.fori_loop(0, planes, two, 0)


GROUPS = 4


def smooth_kernel(n, segments, starts, planes, groups, *refs):
    pieces, refs = refs[:n], refs[n:]
    low, high, before, after, ms_hbm, tile_hbm, s_hbm, a_hbm, t_hbm, out_hbm, g, g1, s, a, t, sems = refs
    count, rows = t.shape[:2]
    ms = g1.at[pl.ds(0, count), pl.ds(0, rows)]
    framed, step = g.shape[0] // GROUPS, count // GROUPS
    ms_copy = pltpu.make_async_copy(ms_hbm, ms, sems.at[0, 0])
    inside = g.at[pl.ds(RIM, count), pl.ds(PAD, rows)]
    g_copy = pltpu.make_async_copy(tile_hbm, inside, sems.at[0, 1])
    ms_copy.start()
    g_copy.start()
    arrivals = []
    for k in range(GROUPS):
        part = pl.ds(k * framed, framed)
        arrivals.append(
            [
                pltpu.make_async_copy(s_hbm.at[part], s.at[part], sems.at[1, k]),
                pltpu.make_async_copy(a_hbm.at[part], a.at[part], sems.at[2, k]),
            ]
        )
    t_copies = []
    for k in range(GROUPS):
        part = pl.ds(k * step, step)
        t_copies.append(pltpu.make_async_copy(t_hbm.at[part], t.at[part], sems.at[3, k]))
    for c in arrivals[0]:
        c.start()
    g[:RIM] = low[...]
    g[count + RIM :] = high[...]
    zero = jnp.zeros((PAD, g.shape[2]), jnp.float32)

    def rims(p, _):
        at = p + RIM
        g[at, :PAD] = zero
        g[at, PAD + rows :] = zero
        g[at, PAD - RIM : PAD] = before[p]
        g[at, PAD + rows : PAD + rows + RIM] = after[p]
        return 0

    lax.fori_loop(0, count, rims, 0)
    ms_copy.wait()
    g_copy.wait()
    for c in sum(arrivals[1:], []) + t_copies:
        c.start()
    place(pieces, segments, starts, planes, groups, ms, g, RIM, PAD)

    def first(p, _):
        for r, m in [(0, PAD), *chunks(rows), (PAD + rows, PAD)]:
            here, total = neighbours(g, p, r, m)
            w = s[p, r : r + m]
            g1[p, r : r + m] = a[p, r : r + m] * here + smoothing_rate * w * w * total
        return 0

    for k in range(GROUPS):
        for c in arrivals[k]:
            c.wait()
        lax.fori_loop(max(1, k * framed), min(g.shape[0] - 1, (k + 1) * framed), first, 0)

    def second(p, _):
        for r, m in chunks(rows):
            here, total = neighbours(g1, p + RIM, r, m)
            t[p, r - PAD : r - PAD + m] = (
                t[p, r - PAD : r - PAD + m] * here + smoothing_rate * s[p + RIM, r : r + m] * total
            )
        return 0

    leaving = []
    for k in range(GROUPS):
        t_copies[k].wait()
        lax.fori_loop(k * step, (k + 1) * step, second, 0)
        part = pl.ds(k * step, step)
        leaving.append(pltpu.make_async_copy(t.at[part], out_hbm.at[part], sems.at[4, k]))
        leaving[-1].start()
    for c in leaving:
        c.wait()


def halo(low, high, axis):
    size = lax.axis_size(axis)
    up = [(i, i + 1) for i in range(size - 1)]
    return lax.ppermute(high, axis, up), lax.ppermute(low, axis, [(j, i) for i, j in up])


def with_rims(tile, before, after):
    planes, rows, depth = tile.shape
    rim = held((RIM, rows + 2 * PAD, depth))
    return pl.pallas_call(
        rim_kernel,
        out_shape=(held((planes + 2 * RIM, rows + 2 * PAD, depth)), rim, rim),
        in_specs=vmem(3),
        out_specs=vmem(3),
        compiler_params=big,
        name="rims",
    )(*hold(tile, before, after))


def shards(source_grad, adjoint_grad, log_model, surface_depth, source_columns, receiver_columns):
    tile_x, tile_y, depth_cells = log_model.shape
    me = lax.axis_index("source")
    y, half = me % 4, me // 4
    lists = block_lists(tile_x, tile_y)
    planes, groups = tables(sum(lists, []))
    parts = [len(blocks) // 8 for blocks in lists]
    after_rest = lax.optimization_barrier

    def start_of(k, offset, z):
        return 8 * sum(parts[:k]) + (2 * ((y + offset) % 4) + z) * parts[k]

    def sums_of(k):
        at = functools.partial(start_of, k)
        starts = [at(2, 1), at(1, 0), at(2, 0), at(-1, 1), at(-1, 0), at(1, 1), at(0, 0), at(0, 1)]
        return partials(source_grad, adjoint_grad, planes, groups, starts, parts[k])

    def first_step(up, down):
        return send(up, UP), send(down, DOWN)

    def second_step(up, down, keep):
        return keep[0] + down[0], keep[1] + up[0]

    def finish(own, up, down, end0, end1):
        own0 = own[0] + up[1] + end0
        own1 = own[1] + down[1] + end1
        return jnp.where(half == 0, own0, own1), jnp.where(half == 0, own1, own0)

    def normalised(own, other):
        total = own + other
        return total[0] * lax.rsqrt(total[1] + floor_eps)

    def ring(piece):
        return [piece, send(piece, UP), send(piece, DOWN), send(piece, ACROSS)]

    ring_offsets = (0, -1, 1, 2)

    up, down, keep, own = sums_of(0)
    log_model, up = after_rest((log_model, up))
    up, down = first_step(up, down)
    depth_index = lax.broadcasted_iota(jnp.int32, (tile_x, tile_y, depth_cells), 2)
    total_y = tile_y * lax.axis_size("line")
    columns = jnp.concatenate([source_columns, receiver_columns])
    electrode_x = columns // total_y
    electrode_y = columns % total_y
    global_x = lax.broadcasted_iota(jnp.int32, (1, tile_x), 1) + lax.axis_index("profile") * tile_x
    global_y = lax.broadcasted_iota(jnp.int32, (1, tile_y), 1) + lax.axis_index("line") * tile_y
    near_x = (jnp.abs(global_x - electrode_x[:, None]) <= mark_radius).astype(jnp.float32)
    near_y = (jnp.abs(global_y - electrode_y[:, None]) <= mark_radius).astype(jnp.float32)
    covered = jnp.einsum("ex,ey->xy", near_x, near_y, precision=lax.Precision.HIGHEST)
    threshold = surface_depth + jnp.where(covered > 0.5, depth_cells // 16, 0)
    root = support_width * lax.rsqrt(log_model * log_model + support_width * support_width)
    root = jnp.where(depth_index >= surface_depth[:, :, None], root, 0.0)
    masked = jnp.where(depth_index >= threshold[:, :, None], root, 0.0)
    up, down, root, masked = after_rest((up, down, root, masked))
    end0, end1 = second_step(up, down, keep)
    source_grad, adjoint_grad, end0, end1 = after_rest((source_grad, adjoint_grad, end0, end1))
    end0, end1 = send(end0, DOWN), send(end1, UP)

    up2, down2, keep2, own2 = sums_of(1)
    own, leaving = finish(own, up, down, end0, end1)
    up2, down2, leaving = after_rest((up2, down2, leaving))
    other = send(leaving, SWAP)
    up, down = first_step(up2, down2)
    end0, end1 = second_step(up, down, keep2)
    source_grad, adjoint_grad, end0, end1, other = after_rest((source_grad, adjoint_grad, end0, end1, other))
    end0, end1 = send(end0, DOWN), send(end1, UP)

    up3, down3, keep3, own3 = sums_of(2)
    own2, leaving = finish(own2, up, down, end0, end1)
    up3, down3, leaving, root = after_rest((up3, down3, leaving, root))
    other2 = send(leaving, SWAP)
    up, down = first_step(up3, down3)
    before, after = halo(root[:, :RIM], root[:, -RIM:], "line")
    wide, low, high = with_rims(root, before, after)
    low, high = halo(low, high, "profile")
    s, a, t = pl.pallas_call(
        coefficient_kernel,
        out_shape=(held(wide.shape),) * 2 + (held(log_model.shape),),
        in_specs=vmem(3),
        out_specs=vmem(3),
        compiler_params=big,
        name="coefficients",
    )(*hold(wide, low, high))
    up, down, wide, other2 = after_rest((up, down, wide, other2))
    end0, end1 = second_step(up, down, keep3)
    end0, end1 = send(end0, DOWN), send(end1, UP)
    frame = jnp.concatenate([normalised(own, other), normalised(own2, other2)])
    frame_other = send(frame, SWAP)
    frame_ring = ring(frame)
    end0, end1, frame_other, s, a, t = after_rest((end0, end1, frame_other, s, a, t))
    own3, leaving = finish(own3, up, down, end0, end1)
    inner = normalised(own3, send(leaving, SWAP))
    inner_other = send(inner, SWAP)
    other_ring = ring(frame_other)
    inner_rings = ring(inner) + ring(inner_other)

    def segments_of(ranges):
        segments = [(i, offset, parts[k]) for i, piece in enumerate(ranges) for k, _, offset, _ in piece]
        starts = jnp.stack([start_of(k, q, z) for piece in ranges for k, z, _, q in piece])
        return segments, starts.astype(jnp.int32)

    pieces = frame_ring + other_ring
    segments, starts = segments_of([[(0, z, 0, q), (1, z, parts[0], q)] for z in (half, 1 - half) for q in ring_offsets])
    rim_y, rim_x = held((tile_x, RIM, depth_cells)), held((RIM, tile_y, depth_cells))
    g, low, high, first, last = pl.pallas_call(
        functools.partial(frame_kernel, len(pieces), segments),
        out_shape=(jax.ShapeDtypeStruct(log_model.shape, jnp.float32), rim_y, rim_y, rim_x, rim_x),
        in_specs=smem(3) + vmem(len(pieces) + 1),
        out_specs=vmem(5),
        compiler_params=big,
        name="frame",
    )(starts, planes, groups, *hold(*pieces, masked))
    before, after = halo(low, high, "line")
    low, high = pl.pallas_call(
        corner_kernel,
        out_shape=(held((RIM, tile_y + 2 * PAD, depth_cells)),) * 2,
        in_specs=vmem(4),
        out_specs=vmem(2),
        compiler_params=big,
        name="corners",
    )(*hold(first, last, before, after))
    low, high = halo(low, high, "profile")
    pieces = inner_rings
    segments, starts = segments_of(
        [[(2, z, 0, q)] for z in (half, 1 - half) for q in ring_offsets]
    )
    wide_f32, tile_f32 = pltpu.VMEM(s.shape, jnp.float32), pltpu.VMEM(log_model.shape, jnp.float32)
    anywhere = pl.BlockSpec(memory_space=pl.ANY)
    return pl.pallas_call(
        functools.partial(smooth_kernel, len(pieces), segments),
        out_shape=jax.ShapeDtypeStruct(log_model.shape, jnp.float32),
        in_specs=smem(3) + vmem(len(pieces) + 4) + [anywhere] * 5,
        out_specs=anywhere,
        scratch_shapes=[wide_f32, wide_f32, wide_f32, wide_f32, tile_f32]
        + [pltpu.SemaphoreType.DMA((5, GROUPS))],
        compiler_params=pltpu.CompilerParams(vmem_limit_bytes=30 * 2**20),
        name="smooth",
    )(starts, planes, groups, *hold(*pieces, low, high, before, after), *in_hbm(masked, g, s, a, t))


def solution(mesh):
    placed = (
        P("source", None, "profile", "line", None),
        P("source", None, "profile", "line", None),
        P("profile", "line", None),
        P("profile", "line"),
        P(),
        P(),
    )
    return jax.shard_map(
        shards, mesh=mesh, in_specs=placed, out_specs=P("profile", "line", None), check_vma=False
    )
```
